32 devices in a mesh: groups: 2 (over y), runs: 4 (over z), sub: 2 (over x), pair: 2 (over core).
Axes of the slice: x: 2, y: 2, z: 4, core: 2. Of those that a mesh axis runs over, the one named last changes fastest.
Arguments:
- embeddings: bfloat16 [8192, 1152], P(('groups', 'runs', 'sub', 'pair')), parts along dimension 0, may hold values from -64 to 64, as said below
- block_cluster: int32 [64], P('groups'), parts along dimension 0, may hold values from 0 to 15, never falling along the last dimension, each value on 1 to 8 neighbouring positions
- owner: int32 [32], P('groups'), parts along dimension 0, may hold values from 0 to 15, each once
Outputs:
- density: float32 [8192], P(('groups', 'runs', 'sub', 'pair')), parts along dimension 0
- prototypes: float32 [32, 1152], P(('groups', 'runs'), 'sub'), parts along dimension 0
The draws below stay inside these ranges and needn't reach their ends.
There are 2 independent parts, one for each index of `groups`. The reference program is written for one: setup_inputs(seed, part) draws one part's arguments, and reference() takes and returns one part's arrays. A program takes and returns all parts, laid end to end along the dimension named above; each array names one. Nothing has to cross between parts.
Inputs may be any that keep to these rules, and one draw needn't show every extreme that they name: `embeddings`: values of order one to a few tens, rows of unlike length. `block_cluster`: never falls along the blocks; each cluster names 1 to 8 consecutive blocks, one exactly 8. `owner`: each slot is named by exactly one cluster.
All inputs are finite; a program needn't handle non-finite values.
Results may differ from the reference program's by a relative error of at most 0.0003.
The reference program's roundings to bfloat16 on the way (of `unit`) count: a program that leaves them out, or rounds other values in their place, can miss the bound.
Values may be sent and summed in bfloat16 or wider, within the bound.
A program may use at most 64 MiB of HBM per device.

```python
import math
import jax
import jax.numpy as jnp
import numpy as np
from jax import lax

E = 1152
BLOCK = 128
BLK_RUN = 8
BLOCKS = 32
ROWS = 4096
CLUSTERS = 16


topic_count = 256


def draw_embeddings(key, part):
    key = jax.random.fold_in(key, 11)
    keys = jax.random.split(key, 5)
    topics = jnp.clip(jax.random.normal(keys[0], (topic_count, E), jnp.float32), -4.0, 4.0)
    which = jax.random.randint(keys[1], (ROWS,), 0, topic_count)
    strength = jnp.exp(jax.random.uniform(keys[2], (ROWS, 1), jnp.float32, jnp.log(0.3), jnp.log(3.0)))
    picked = jnp.take(topics, which, axis=0)
    noise = jnp.clip(jax.random.normal(keys[3], (ROWS, E), jnp.float32), -4.0, 4.0)
    scale = jnp.exp(jax.random.uniform(keys[4], (ROWS, 1), jnp.float32, jnp.log(0.5), jnp.log(2.0)))
    return (scale * (strength * picked + noise)).astype(jnp.bfloat16)


def profile(number_of, total, limit, skew):
    weights = [(1 << 20) // math.isqrt(standing ** skew) + 1 for standing in range(2, number_of + 1)]
    rest, holding = total - limit - (number_of - 1), [1] * (number_of - 1)
    while rest > 0:
        movable = [i for i in range(number_of - 1) if holding[i] < limit]
        pool, left = sum([weights[i] for i in movable]), rest
        for i in movable:
            extra = min(limit - holding[i], max(1, left * weights[i] // pool), rest)
            holding[i] = holding[i] + extra
            rest = rest - extra
    return np.array([limit] + holding)


def uneven_parts(key, number_of, total, bound, skew):
    if number_of == 2:
        one = jax.random.randint(key, (), max(1, total - bound), min(bound, total - 1) + 1)
        return jnp.stack([one, total - one])
    tallies = jnp.asarray(profile(number_of, total, bound, skew), jnp.int32)
    couples = (number_of - 1) // 2
    donor, taker = tallies[1:1 + 2 * couples:2], tallies[2:2 + 2 * couples:2]
    slack = jnp.minimum(donor - 1, bound - taker)
    shifted = jax.random.randint(jax.random.fold_in(key, 1), (couples,), 0, 1 << 20) % (slack + 1)
    tallies = tallies.at[1:1 + 2 * couples:2].set(donor - shifted).at[2:2 + 2 * couples:2].set(taker + shifted)
    return tallies[jax.random.permutation(jax.random.fold_in(key, 2), number_of)]


def setup_inputs(seed: int = 0, part: int = 0) -> dict:
    splits = jax.random.split(jax.random.key(seed), 4)
    part_splits = jax.random.split(jax.random.fold_in(splits[3], part), 4)
    embeddings = draw_embeddings(jax.random.fold_in(jax.random.fold_in(splits[3], part), 71), part)
    block_cluster = jnp.searchsorted(jnp.cumsum(uneven_parts(part_splits[1], CLUSTERS, BLOCKS, BLK_RUN, 2)), jnp.arange(BLOCKS), side="right").astype(jnp.int32)
    owner = jax.random.permutation(part_splits[2], CLUSTERS).astype(jnp.int32)
    return dict(embeddings=embeddings, block_cluster=block_cluster, owner=owner)


sharpness = 8.0

def reference(embeddings, block_cluster, owner):
    values = embeddings.astype(jnp.float32)
    unit = (values * lax.rsqrt(lax.optimization_barrier(jnp.mean(values * values, axis=-1, keepdims=True)) + 1e-06)).astype(jnp.bfloat16)
    blocks = block_cluster.shape[0]
    row_ids = jnp.repeat(block_cluster, BLOCK)
    first = jnp.argmax(block_cluster[None, :] == block_cluster[:, None], axis=1).astype(jnp.int32)
    start = jnp.minimum(first, blocks - BLK_RUN).astype(jnp.int32)

    def one_block(index):
        rows = lax.dynamic_slice_in_dim(unit, (index * BLOCK).astype(jnp.int32), BLOCK, 0)
        begin = (start[index] * BLOCK).astype(jnp.int32)
        window = lax.dynamic_slice_in_dim(unit, begin, BLK_RUN * BLOCK, 0)
        window_ids = lax.dynamic_slice_in_dim(row_ids, begin, BLK_RUN * BLOCK, 0)
        dots = jnp.einsum('ie,je->ij', rows, window, preferred_element_type=jnp.float32)
        same = window_ids[None, :] == block_cluster[index]
        terms = jnp.where(same, jnp.exp(sharpness * (dots / E) - sharpness), 0.0)
        return lax.optimization_barrier(jnp.sum(terms, axis=1))
    density = lax.map(one_block, jnp.arange(blocks, dtype=jnp.int32)).reshape(-1)
    weight = 1.0 / density
    block_sum = jnp.einsum('bi,bie->be', weight.reshape(blocks, BLOCK), unit.reshape(blocks, BLOCK, E).astype(jnp.float32), precision=lax.Precision.HIGHEST)
    block_weight = lax.optimization_barrier(jnp.sum(weight.reshape(blocks, BLOCK), axis=1))
    slot = owner[block_cluster]
    place = (slot[:, None] == jnp.arange(CLUSTERS, dtype=jnp.int32)[None, :]).astype(jnp.float32)
    proto_sum = jnp.dot(place.T, block_sum, precision=lax.Precision.HIGHEST)
    weight_total = jnp.dot(block_weight, place, precision=lax.Precision.HIGHEST)
    return (density, proto_sum / weight_total[:, None])
```

```python
import functools

import jax
import jax.numpy as jnp
from jax import lax
from jax.experimental import pallas as pl
from jax.experimental.pallas import tpu as pltpu
from jax.sharding import PartitionSpec as P

BLOCK = 128
SHARPNESS = 8.0
MESH = pl.DeviceIdType.MESH


def kernel(
    sizes,
    x_ref,
    ids_ref,
    owner_ref,
    dens_ref,
    proto_ref,
    slab,
    rx,
    acc,
    ret,
    part,
    msg,
    gathered,
    mate_send,
    mate_recv,
    rows_send,
    rows_recv,
    ret_send,
    part_recv,
    msg_send,
    msg_recv,
):
    n_runs, n_sub, n_pair, blk_dev, lows, lanes, slots = sizes
    rows, width = x_ref.shape
    chips = n_runs * n_sub
    count = chips * n_pair
    blk_chip = blk_dev * n_pair
    run, sub, core = (lax.axis_index(a) for a in ("runs", "sub", "pair"))
    chip = run * n_sub + sub
    me = chip * n_pair + core
    mate = 1 - core

    def at(device_chip, device_core):
        return {
            "runs": device_chip // n_sub,
            "sub": device_chip % n_sub,
            "pair": device_core,
        }

    part[...] = jnp.zeros_like(part)
    acc[...] = jnp.zeros_like(acc)
    ret[...] = jnp.zeros_like(ret)

    barrier = pltpu.get_barrier_semaphore()

    def greet(step, carry):
        other = lax.rem(me + step, count)
        pl.semaphore_signal(
            barrier, inc=1, device_id=at(other // n_pair, other % n_pair), device_id_type=MESH
        )
        return carry

    lax.fori_loop(1, count, greet, 0)

    for b in range(blk_dev):
        span = pl.ds(b * BLOCK, BLOCK)
        values = x_ref[span, :].astype(jnp.float32)
        mean = jnp.sum(values * values, axis=1, keepdims=True) / width
        slab[core, span, :] = (values * lax.rsqrt(mean + 1e-06)).astype(jnp.bfloat16)

    pl.semaphore_wait(barrier, count - 1)

    def target(d):
        return chip + d if d < n_sub else chip - n_sub

    def source(d):
        return chip - d if d < n_sub else chip + n_sub

    def inside(c):
        return (c >= 0) & (c < chips)

    def needed(d, b):
        return (core * blk_dev + b < blk_chip - 1) if d == n_sub else True

    def row_copy(d, b):
        span = pl.ds(b * BLOCK, BLOCK)
        return pltpu.make_async_remote_copy(
            src_ref=slab.at[core, span, :],
            dst_ref=rx.at[d - 1, span, :],
            send_sem=rows_send.at[d - 1, b],
            recv_sem=rows_recv.at[d - 1, b],
            device_id=at(target(d), core),
            device_id_type=MESH,
        )

    steps = [(b, d) for b in range(blk_dev) for d in range(1, n_sub + 1)]
    for b, d in steps:
        @pl.when(inside(target(d)) & needed(d, b))
        def _():
            row_copy(d, b).start()

    mate_copy = pltpu.make_async_remote_copy(
        src_ref=slab.at[core],
        dst_ref=slab.at[core],
        send_sem=mate_send,
        recv_sem=mate_recv,
        device_id=at(chip, mate),
        device_id_type=MESH,
    )
    mate_copy.start()
    mate_arrives = pltpu.make_async_remote_copy(
        src_ref=slab.at[core],
        dst_ref=slab.at[mate],
        send_sem=mate_send,
        recv_sem=mate_recv,
        device_id=at(chip, mate),
        device_id_type=MESH,
    )
    mate_arrives.wait_recv()

    def terms(left, right):
        dots = lax.dot_general(
            left, right, (((1,), (1,)), ((), ())), preferred_element_type=jnp.float32
        )
        return jnp.exp(SHARPNESS * (dots / width) - SHARPNESS)

    def same(left, rights):
        return jnp.concatenate(
            [
                jnp.full((1, BLOCK), jnp.where(ids_ref[r] == ids_ref[left], 1.0, 0.0), jnp.float32)
                for r in rights
            ],
            axis=1,
        )

    own_blocks = [me * blk_dev + b for b in range(blk_dev)]
    chip_blocks = [chip * blk_chip + b for b in range(blk_chip)]

    density = jnp.zeros((1, rows), jnp.float32)
    own = slab[core]
    for j in range(blk_chip):
        c, b = divmod(j, blk_dev)
        t = terms(slab[c, pl.ds(b * BLOCK, BLOCK), :], own)
        density = density + jnp.sum(t, axis=0, keepdims=True) * same(chip_blocks[j], own_blocks)

    def return_copy(d):
        return pltpu.make_async_remote_copy(
            src_ref=ret.at[d - 1],
            dst_ref=part.at[d - 1],
            send_sem=ret_send.at[d - 1],
            recv_sem=part_recv.at[d - 1],
            device_id=at(source(d), core),
            device_id_type=MESH,
        )

    def part_arrives(d):
        return pltpu.make_async_remote_copy(
            src_ref=ret.at[d - 1],
            dst_ref=part.at[d - 1],
            send_sem=ret_send.at[d - 1],
            recv_sem=part_recv.at[d - 1],
            device_id=at(target(d), core),
            device_id_type=MESH,
        )

    for b, d in steps:
        @pl.when(inside(source(d)) & needed(d, b))
        def _():
            row_copy(d, b).wait_recv()
            span = pl.ds(b * BLOCK, BLOCK)
            their = source(d) * blk_chip + core * blk_dev + b
            whole = slab[...].reshape(n_pair * rows, width)
            t = terms(rx[d - 1, span, :], whole) * same(their, chip_blocks)
            down = jnp.sum(t, axis=0, keepdims=True)
            for c in range(n_pair):
                acc[c] += down[:, c * rows:(c + 1) * rows]
            fold = sum(t[:, j * BLOCK:(j + 1) * BLOCK] for j in range(blk_chip))
            ret[d - 1, :, span] = jnp.sum(fold.T, axis=0, keepdims=True)

        if b == blk_dev - 1:
            @pl.when(inside(source(d)))
            def _():
                return_copy(d).start()

    mate_part = pltpu.make_async_remote_copy(
        src_ref=acc.at[mate],
        dst_ref=part.at[n_sub],
        send_sem=ret_send.at[n_sub],
        recv_sem=part_recv.at[n_sub],
        device_id=at(chip, mate),
        device_id_type=MESH,
    )
    mate_part.start()
    density = density + acc[core]
    mate_part.wait_recv()
    for d in range(1, n_sub + 1):
        @pl.when(inside(target(d)))
        def _():
            part_arrives(d).wait_recv()
    for d in range(n_sub + 1):
        density = density + part[d]
    dens_ref[...] = density

    weight = 1.0 / density
    lane = lax.broadcasted_iota(jnp.int32, (1, rows), 1)
    hi = weight.astype(jnp.bfloat16).astype(jnp.float32)
    mid = (weight - hi).astype(jnp.bfloat16).astype(jnp.float32)
    low = weight - hi - mid
    left = jnp.concatenate(
        [
            jnp.where(lane // BLOCK == b, piece, 0.0)
            for piece in (hi, mid, low)
            for b in range(blk_dev)
        ],
        axis=0,
    ).astype(jnp.bfloat16)
    sums = jnp.dot(left, own, preferred_element_type=jnp.float32)
    sums = (
        sums[0:blk_dev] + sums[blk_dev:2 * blk_dev] + sums[2 * blk_dev:3 * blk_dev]
    )
    totals = jnp.concatenate(
        [
            jnp.sum(weight[:, b * BLOCK:(b + 1) * BLOCK], axis=1, keepdims=True)
            for b in range(blk_dev)
        ],
        axis=0,
    )
    for s in range(n_sub):
        msg[s, :, pl.ds(0, lanes)] = sums[:, lows[s]:lows[s] + lanes]
        msg[s, :, pl.ds(lanes, 128)] = jnp.broadcast_to(totals, (blk_dev, 128))

    def spread(step, carry):
        other = lax.rem(me + step, count)
        other_chip = other // n_pair
        pltpu.make_async_remote_copy(
            src_ref=msg.at[other_chip % n_sub],
            dst_ref=gathered.at[me],
            send_sem=msg_send,
            recv_sem=msg_recv,
            device_id=at(other_chip, other % n_pair),
            device_id_type=MESH,
        ).start()
        return carry

    lax.fori_loop(1, count, spread, 0)
    gathered[me] = msg[sub]

    mate_copy.wait_send()
    mate_part.wait_send()
    for b, d in steps:
        @pl.when(inside(target(d)) & needed(d, b))
        def _():
            row_copy(d, b).wait_send()
    for d in range(1, n_sub + 1):
        @pl.when(inside(source(d)))
        def _():
            return_copy(d).wait_send()

    most = gathered.at[pl.ds(0, count - 1)]
    pltpu.make_async_copy(most, most, msg_recv).wait()

    slot_row = lax.broadcasted_iota(jnp.int32, (8, 1), 0) + run * slots

    def place(q, total):
        got = gathered[q]
        for b in range(blk_dev):
            slot = owner_ref[ids_ref[q * blk_dev + b]]
            total = total + jnp.where(slot_row == slot, got[b:b + 1, :], 0.0)
        return total

    total = lax.fori_loop(
        0, count, place, jnp.zeros((8, lanes + 128), jnp.float32), unroll=4
    )
    proto_ref[...] = (total[:, 0:lanes] / total[:, lanes:lanes + 1])[0:slots]
    pltpu.make_async_copy(most, most, msg_send).wait()


def per_device(sizes, embeddings, block_cluster, owner):
    n_runs, n_sub, n_pair, blk_dev, lows, lanes, slots = sizes
    rows, width = embeddings.shape
    count = n_runs * n_sub * n_pair
    vmem = pl.BlockSpec(memory_space=pltpu.VMEM)
    smem = pl.BlockSpec(memory_space=pltpu.SMEM)
    density, wide = pl.pallas_call(
        functools.partial(kernel, sizes),
        out_shape=(
            jax.ShapeDtypeStruct((1, rows), jnp.float32),
            jax.ShapeDtypeStruct((slots, lanes), jnp.float32),
        ),
        in_specs=[vmem, smem, smem],
        out_specs=(vmem, vmem),
        scratch_shapes=[
            pltpu.VMEM((n_pair, rows, width), jnp.bfloat16),
            pltpu.VMEM((n_sub, rows, width), jnp.bfloat16),
            pltpu.VMEM((n_pair, 1, rows), jnp.float32),
            pltpu.VMEM((n_sub, 1, rows), jnp.float32),
            pltpu.VMEM((n_sub + 1, 1, rows), jnp.float32),
            pltpu.VMEM((n_sub, blk_dev, lanes + 128), jnp.float32),
            pltpu.VMEM((count, blk_dev, lanes + 128), jnp.float32),
            pltpu.SemaphoreType.DMA,
            pltpu.SemaphoreType.DMA,
            pltpu.SemaphoreType.DMA((n_sub, blk_dev)),
            pltpu.SemaphoreType.DMA((n_sub, blk_dev)),
            pltpu.SemaphoreType.DMA((n_sub + 1,)),
            pltpu.SemaphoreType.DMA((n_sub + 1,)),
            pltpu.SemaphoreType.DMA,
            pltpu.SemaphoreType.DMA,
        ],
        compiler_params=pltpu.CompilerParams(
            collective_id=0, has_side_effects=True, vmem_limit_bytes=32 * 1024 * 1024
        ),
    )(embeddings, block_cluster, owner)
    sub = lax.axis_index("sub")
    feature_width = width // n_sub
    offset = sub * feature_width - jnp.asarray(lows, jnp.int32)[sub]
    return (density.reshape(rows), lax.dynamic_slice_in_dim(wide, offset, feature_width, 1))


def solution(mesh):
    placed = (P(("groups", "runs", "sub", "pair"), None), P("groups"), P("groups"))

    def whole(embeddings, block_cluster, owner):
        n_runs, n_sub, n_pair = (mesh.shape[a] for a in ("runs", "sub", "pair"))
        groups = mesh.shape["groups"]
        rows = embeddings.shape[0] // mesh.size
        width = embeddings.shape[1]
        feature_width = width // n_sub
        spans = [
            (s * feature_width // 128 * 128, -(-((s + 1) * feature_width) // 128) * 128)
            for s in range(n_sub)
        ]
        lanes = max(hi - lo for lo, hi in spans)
        lows = tuple(min(lo, width - lanes) for lo, _ in spans)
        slots = owner.shape[0] // groups // n_runs
        sizes = (n_runs, n_sub, n_pair, rows // BLOCK, lows, lanes, slots)
        return jax.shard_map(
            functools.partial(per_device, sizes),
            mesh=mesh,
            in_specs=placed,
            out_specs=(P(("groups", "runs", "sub", "pair")), P(("groups", "runs"), "sub")),
            check_vma=False,
        )(embeddings, block_cluster, owner)

    return whole
```

```python
import functools

import jax
import jax.numpy as jnp
from jax import lax
from jax.experimental import pallas as pl
from jax.experimental.pallas import tpu as pltpu
from jax.sharding import PartitionSpec as P

BLOCK = 128
SHARPNESS = 8.0
MESH = pl.DeviceIdType.MESH


def kernel(
    sizes,
    x_hbm,
    ids_hbm,
    owner_hbm,
    dens_ref,
    proto_ref,
    x_ref,
    ids_ref,
    owner_ref,
    slab,
    rx,
    acc,
    ret,
    part,
    msg,
    gathered,
    load_sem,
    near,
    mate_send,
    mate_recv,
    rows_send,
    rows_recv,
    ret_send,
    part_recv,
    msg_send,
    msg_recv,
):
    n_runs, n_sub, n_pair, blk_dev, lows, lanes, slots = sizes
    rows, width = x_hbm.shape
    chips = n_runs * n_sub
    count = chips * n_pair
    blk_chip = blk_dev * n_pair
    run, sub, core = (lax.axis_index(a) for a in ("runs", "sub", "pair"))
    chip = run * n_sub + sub
    me = chip * n_pair + core
    mate = 1 - core

    def at(device_chip, device_core):
        return {
            "runs": device_chip // n_sub,
            "sub": device_chip % n_sub,
            "pair": device_core,
        }

    loads = [
        pltpu.make_async_copy(
            x_hbm.at[pl.ds(b * BLOCK, BLOCK)],
            x_ref.at[pl.ds(b * BLOCK, BLOCK)],
            load_sem.at[b],
        )
        for b in range(blk_dev)
    ]
    loads.append(pltpu.make_async_copy(ids_hbm, ids_ref, load_sem.at[blk_dev]))
    loads.append(pltpu.make_async_copy(owner_hbm, owner_ref, load_sem.at[blk_dev + 1]))

    part[...] = jnp.zeros_like(part)

    barrier = pltpu.get_barrier_semaphore()
    away = [d for step in range(1, n_sub + 1) for d in (step, -step)]

    def inside(c):
        return (c >= 0) & (c < chips)

    def greet(semaphore):
        pl.semaphore_signal(semaphore, inc=1, device_id=at(chip, mate), device_id_type=MESH)
        for d in away:
            @pl.when(inside(chip + d))
            def _():
                pl.semaphore_signal(
                    semaphore, inc=1, device_id=at(chip + d, core), device_id_type=MESH
                )

    known = 1 + sum(jnp.where(inside(chip + d), 1, 0) for d in away)
    greet(barrier)
    for load in loads:
        load.start()
    acc[...] = jnp.zeros_like(acc)
    ret[...] = jnp.zeros_like(ret)

    for b in range(blk_dev):
        span = pl.ds(b * BLOCK, BLOCK)
        loads[b].wait()
        values = x_ref[span, :].astype(jnp.float32)
        mean = jnp.sum(values * values, axis=1, keepdims=True) / width
        slab[core, span, :] = (values * lax.rsqrt(mean + 1e-06)).astype(jnp.bfloat16)

    pl.semaphore_wait(barrier, known)

    def target(d):
        return chip + d if d < n_sub else chip - n_sub

    def source(d):
        return chip - d if d < n_sub else chip + n_sub

    def needed(d, b):
        return (core * blk_dev + b < blk_chip - 1) if d == n_sub else True

    def row_copy(d, b):
        span = pl.ds(b * BLOCK, BLOCK)
        return pltpu.make_async_remote_copy(
            src_ref=slab.at[core, span, :],
            dst_ref=rx.at[d - 1, span, :],
            send_sem=rows_send.at[d - 1, b],
            recv_sem=rows_recv.at[d - 1, b],
            device_id=at(target(d), core),
            device_id_type=MESH,
        )

    steps = [(b, d) for b in range(blk_dev) for d in range(1, n_sub + 1)]
    for b, d in steps:
        @pl.when(inside(target(d)) & needed(d, b))
        def _():
            row_copy(d, b).start()

    mate_copy = pltpu.make_async_remote_copy(
        src_ref=slab.at[core],
        dst_ref=slab.at[core],
        send_sem=mate_send,
        recv_sem=mate_recv,
        device_id=at(chip, mate),
        device_id_type=MESH,
    )
    mate_copy.start()
    loads[blk_dev].wait()
    loads[blk_dev + 1].wait()
    mate_arrives = pltpu.make_async_remote_copy(
        src_ref=slab.at[core],
        dst_ref=slab.at[mate],
        send_sem=mate_send,
        recv_sem=mate_recv,
        device_id=at(chip, mate),
        device_id_type=MESH,
    )
    mate_arrives.wait_recv()

    def terms(left, right):
        dots = lax.dot_general(
            left, right, (((1,), (1,)), ((), ())), preferred_element_type=jnp.float32
        )
        return jnp.exp(SHARPNESS * (dots / width) - SHARPNESS)

    def same(left, rights):
        return jnp.concatenate(
            [
                jnp.full((1, BLOCK), jnp.where(ids_ref[r] == ids_ref[left], 1.0, 0.0), jnp.float32)
                for r in rights
            ],
            axis=1,
        )

    own_blocks = [me * blk_dev + b for b in range(blk_dev)]
    chip_blocks = [chip * blk_chip + b for b in range(blk_chip)]

    def hop(step, carry):
        greet(near.at[step])
        pl.semaphore_wait(near.at[step], known)
        return carry

    density = jnp.zeros((1, rows), jnp.float32)
    own = slab[core]
    for j in range(blk_chip):
        c, b = divmod(j, blk_dev)
        t = terms(slab[c, pl.ds(b * BLOCK, BLOCK), :], own)
        density = density + jnp.sum(t, axis=0, keepdims=True) * same(chip_blocks[j], own_blocks)

    lax.fori_loop(0, near.shape[0], hop, 0)

    def return_copy(d):
        return pltpu.make_async_remote_copy(
            src_ref=ret.at[d - 1],
            dst_ref=part.at[d - 1],
            send_sem=ret_send.at[d - 1],
            recv_sem=part_recv.at[d - 1],
            device_id=at(source(d), core),
            device_id_type=MESH,
        )

    def part_arrives(d):
        return pltpu.make_async_remote_copy(
            src_ref=ret.at[d - 1],
            dst_ref=part.at[d - 1],
            send_sem=ret_send.at[d - 1],
            recv_sem=part_recv.at[d - 1],
            device_id=at(target(d), core),
            device_id_type=MESH,
        )

    for b, d in steps:
        @pl.when(inside(source(d)) & needed(d, b))
        def _():
            row_copy(d, b).wait_recv()
            span = pl.ds(b * BLOCK, BLOCK)
            their = source(d) * blk_chip + core * blk_dev + b
            whole = slab[...].reshape(n_pair * rows, width)
            t = terms(rx[d - 1, span, :], whole) * same(their, chip_blocks)
            down = jnp.sum(t, axis=0, keepdims=True)
            for c in range(n_pair):
                acc[c] += down[:, c * rows:(c + 1) * rows]
            fold = sum(t[:, j * BLOCK:(j + 1) * BLOCK] for j in range(blk_chip))
            ret[d - 1, :, span] = jnp.sum(fold.T, axis=0, keepdims=True)

        if b == blk_dev - 1:
            @pl.when(inside(source(d)))
            def _():
                return_copy(d).start()

    mate_part = pltpu.make_async_remote_copy(
        src_ref=acc.at[mate],
        dst_ref=part.at[n_sub],
        send_sem=ret_send.at[n_sub],
        recv_sem=part_recv.at[n_sub],
        device_id=at(chip, mate),
        device_id_type=MESH,
    )
    mate_part.start()
    density = density + acc[core]
    mate_part.wait_recv()
    for d in range(1, n_sub + 1):
        @pl.when(inside(target(d)))
        def _():
            part_arrives(d).wait_recv()
    for d in range(n_sub + 1):
        density = density + part[d]
    dens_ref[...] = density

    weight = 1.0 / density
    lane = lax.broadcasted_iota(jnp.int32, (1, rows), 1)
    hi = weight.astype(jnp.bfloat16).astype(jnp.float32)
    mid = (weight - hi).astype(jnp.bfloat16).astype(jnp.float32)
    low = weight - hi - mid
    left = jnp.concatenate(
        [
            jnp.where(lane // BLOCK == b, piece, 0.0)
            for piece in (hi, mid, low)
            for b in range(blk_dev)
        ],
        axis=0,
    ).astype(jnp.bfloat16)
    sums = jnp.dot(left, own, preferred_element_type=jnp.float32)
    sums = (
        sums[0:blk_dev] + sums[blk_dev:2 * blk_dev] + sums[2 * blk_dev:3 * blk_dev]
    )
    totals = jnp.concatenate(
        [
            jnp.sum(weight[:, b * BLOCK:(b + 1) * BLOCK], axis=1, keepdims=True)
            for b in range(blk_dev)
        ],
        axis=0,
    )
    for s in range(n_sub):
        msg[s, :, pl.ds(0, lanes)] = sums[:, lows[s]:lows[s] + lanes]
        msg[s, :, pl.ds(lanes, 128)] = jnp.broadcast_to(totals, (blk_dev, 128))

    def spread(step, carry):
        other = lax.rem(me + step, count)
        other_chip = other // n_pair
        pltpu.make_async_remote_copy(
            src_ref=msg.at[other_chip % n_sub],
            dst_ref=gathered.at[me],
            send_sem=msg_send,
            recv_sem=msg_recv,
            device_id=at(other_chip, other % n_pair),
            device_id_type=MESH,
        ).start()
        return carry

    lax.fori_loop(1, count, spread, 0)
    gathered[me] = msg[sub]

    mate_copy.wait_send()
    mate_part.wait_send()
    for b, d in steps:
        @pl.when(inside(target(d)) & needed(d, b))
        def _():
            row_copy(d, b).wait_send()
    for d in range(1, n_sub + 1):
        @pl.when(inside(source(d)))
        def _():
            return_copy(d).wait_send()

    most = gathered.at[pl.ds(0, count - 1)]
    pltpu.make_async_copy(most, most, msg_recv).wait()

    slot_row = lax.broadcasted_iota(jnp.int32, (8, 1), 0) + run * slots

    def place(q, total):
        got = gathered[q]
        for b in range(blk_dev):
            slot = owner_ref[ids_ref[q * blk_dev + b]]
            total = total + jnp.where(slot_row == slot, got[b:b + 1, :], 0.0)
        return total

    total = lax.fori_loop(
        0, count, place, jnp.zeros((8, lanes + 128), jnp.float32), unroll=4
    )
    proto_ref[...] = (total[:, 0:lanes] / total[:, lanes:lanes + 1])[0:slots]
    pltpu.make_async_copy(most, most, msg_send).wait()


def per_device(sizes, embeddings, block_cluster, owner):
    n_runs, n_sub, n_pair, blk_dev, lows, lanes, slots = sizes
    rows, width = embeddings.shape
    count = n_runs * n_sub * n_pair
    vmem = pl.BlockSpec(memory_space=pltpu.VMEM)
    hops = -(-(n_runs * n_sub - 1) // n_sub)
    density, wide = pl.pallas_call(
        functools.partial(kernel, sizes),
        out_shape=(
            jax.ShapeDtypeStruct((1, rows), jnp.float32),
            jax.ShapeDtypeStruct((slots, lanes), jnp.float32),
        ),
        in_specs=[pl.BlockSpec(memory_space=pl.ANY)] * 3,
        out_specs=(vmem, vmem),
        scratch_shapes=[
            pltpu.VMEM((rows, width), jnp.bfloat16),
            pltpu.SMEM(block_cluster.shape, jnp.int32),
            pltpu.SMEM(owner.shape, jnp.int32),
            pltpu.VMEM((n_pair, rows, width), jnp.bfloat16),
            pltpu.VMEM((n_sub, rows, width), jnp.bfloat16),
            pltpu.VMEM((n_pair, 1, rows), jnp.float32),
            pltpu.VMEM((n_sub, 1, rows), jnp.float32),
            pltpu.VMEM((n_sub + 1, 1, rows), jnp.float32),
            pltpu.VMEM((n_sub, blk_dev, lanes + 128), jnp.float32),
            pltpu.VMEM((count, blk_dev, lanes + 128), jnp.float32),
            pltpu.SemaphoreType.DMA((blk_dev + 2,)),
            pltpu.SemaphoreType.REGULAR((hops,)),
            pltpu.SemaphoreType.DMA,
            pltpu.SemaphoreType.DMA,
            pltpu.SemaphoreType.DMA((n_sub, blk_dev)),
            pltpu.SemaphoreType.DMA((n_sub, blk_dev)),
            pltpu.SemaphoreType.DMA((n_sub + 1,)),
            pltpu.SemaphoreType.DMA((n_sub + 1,)),
            pltpu.SemaphoreType.DMA,
            pltpu.SemaphoreType.DMA,
        ],
        compiler_params=pltpu.CompilerParams(
            collective_id=0, has_side_effects=True, vmem_limit_bytes=32 * 1024 * 1024
        ),
    )(embeddings, block_cluster, owner)
    sub = lax.axis_index("sub")
    feature_width = width // n_sub
    offset = sub * feature_width - jnp.asarray(lows, jnp.int32)[sub]
    return (density.reshape(rows), lax.dynamic_slice_in_dim(wide, offset, feature_width, 1))


def solution(mesh):
    placed = (P(("groups", "runs", "sub", "pair"), None), P("groups"), P("groups"))

    def whole(embeddings, block_cluster, owner):
        n_runs, n_sub, n_pair = (mesh.shape[a] for a in ("runs", "sub", "pair"))
        groups = mesh.shape["groups"]
        rows = embeddings.shape[0] // mesh.size
        width = embeddings.shape[1]
        feature_width = width // n_sub
        spans = [
            (s * feature_width // 128 * 128, -(-((s + 1) * feature_width) // 128) * 128)
            for s in range(n_sub)
        ]
        lanes = max(hi - lo for lo, hi in spans)
        lows = tuple(min(lo, width - lanes) for lo, _ in spans)
        slots = owner.shape[0] // groups // n_runs
        sizes = (n_runs, n_sub, n_pair, rows // BLOCK, lows, lanes, slots)
        return jax.shard_map(
            functools.partial(per_device, sizes),
            mesh=mesh,
            in_specs=placed,
            out_specs=(P(("groups", "runs", "sub", "pair")), P(("groups", "runs"), "sub")),
            check_vma=False,
        )(embeddings, block_cluster, owner)

    return whole
```

```python
import functools

import jax
import jax.numpy as jnp
from jax import lax
from jax.experimental import pallas as pl
from jax.experimental.pallas import tpu as pltpu
from jax.sharding import PartitionSpec as P

BLOCK = 128
SHARPNESS = 8.0
MESH = pl.DeviceIdType.MESH


def kernel(
    sizes,
    x_hbm,
    ids_hbm,
    owner_hbm,
    dens_ref,
    proto_ref,
    x_ref,
    ids_ref,
    owner_ref,
    slab,
    rx,
    acc,
    ret,
    part,
    msg,
    gathered,
    load_sem,
    near,
    mate_send,
    mate_recv,
    rows_send,
    rows_recv,
    ret_send,
    part_recv,
    msg_send,
    msg_recv,
):
    n_runs, n_sub, n_pair, blk_dev, lows, lanes, slots = sizes
    rows, width = x_hbm.shape
    feature_width = width // n_sub
    chips = n_runs * n_sub
    count = chips * n_pair
    blk_chip = blk_dev * n_pair
    run, sub, core = (lax.axis_index(a) for a in ("runs", "sub", "pair"))
    chip = run * n_sub + sub
    me = chip * n_pair + core
    mate = 1 - core

    def at(device_chip, device_core):
        return {
            "runs": device_chip // n_sub,
            "sub": device_chip % n_sub,
            "pair": device_core,
        }

    loads = [
        pltpu.make_async_copy(
            x_hbm.at[pl.ds(b * BLOCK, BLOCK)],
            x_ref.at[pl.ds(b * BLOCK, BLOCK)],
            load_sem.at[b],
        )
        for b in range(blk_dev)
    ]
    loads.append(pltpu.make_async_copy(ids_hbm, ids_ref, load_sem.at[blk_dev]))
    loads.append(pltpu.make_async_copy(owner_hbm, owner_ref, load_sem.at[blk_dev + 1]))

    part[...] = jnp.zeros_like(part)

    barrier = pltpu.get_barrier_semaphore()
    away = [d for step in range(1, n_sub + 1) for d in (step, -step)]

    def inside(c):
        return (c >= 0) & (c < chips)

    def greet(semaphore):
        pl.semaphore_signal(semaphore, inc=1, device_id=at(chip, mate), device_id_type=MESH)
        for d in away:
            @pl.when(inside(chip + d))
            def _():
                pl.semaphore_signal(
                    semaphore, inc=1, device_id=at(chip + d, core), device_id_type=MESH
                )

    known = 1 + sum(jnp.where(inside(chip + d), 1, 0) for d in away)
    greet(barrier)
    for load in loads:
        load.start()

    def target(d):
        return chip + d if d < n_sub else chip - n_sub

    def source(d):
        return chip - d if d < n_sub else chip + n_sub

    def needed(d, b):
        return (core * blk_dev + b < blk_chip - 1) if d == n_sub else True

    def row_copy(d, b):
        span = pl.ds(b * BLOCK, BLOCK)
        return pltpu.make_async_remote_copy(
            src_ref=x_hbm.at[span, :],
            dst_ref=rx.at[d - 1, span, :],
            send_sem=rows_send.at[d - 1, b],
            recv_sem=rows_recv.at[d - 1, b],
            device_id=at(target(d), core),
            device_id_type=MESH,
        )

    starts = [(b, d) for d in range(1, n_sub + 1) for b in range(blk_dev)]
    steps = [(b, d) for b in range(blk_dev) for d in range(n_sub, 0, -1)]
    pl.semaphore_wait(barrier, known)
    for b, d in starts:
        @pl.when(inside(target(d)) & needed(d, b))
        def _():
            row_copy(d, b).start()

    def normal(values):
        values = values.astype(jnp.float32)
        mean = jnp.sum(values * values, axis=1, keepdims=True) / width
        return (values * lax.rsqrt(mean + 1e-06)).astype(jnp.bfloat16)

    acc[...] = jnp.zeros_like(acc)
    ret[...] = jnp.zeros_like(ret)
    for b in range(blk_dev):
        span = pl.ds(b * BLOCK, BLOCK)
        loads[b].wait()
        slab[core, span, :] = normal(x_ref[span, :])

    mate_copy = pltpu.make_async_remote_copy(
        src_ref=slab.at[core],
        dst_ref=slab.at[core],
        send_sem=mate_send,
        recv_sem=mate_recv,
        device_id=at(chip, mate),
        device_id_type=MESH,
    )
    mate_copy.start()
    loads[blk_dev].wait()
    loads[blk_dev + 1].wait()
    mate_arrives = pltpu.make_async_remote_copy(
        src_ref=slab.at[core],
        dst_ref=slab.at[mate],
        send_sem=mate_send,
        recv_sem=mate_recv,
        device_id=at(chip, mate),
        device_id_type=MESH,
    )
    mate_arrives.wait_recv()

    def terms(left, right):
        dots = lax.dot_general(
            left, right, (((1,), (1,)), ((), ())), preferred_element_type=jnp.float32
        )
        return jnp.exp(SHARPNESS * (dots / width) - SHARPNESS)

    def same(left, rights):
        return jnp.concatenate(
            [
                jnp.full((1, BLOCK), jnp.where(ids_ref[r] == ids_ref[left], 1.0, 0.0), jnp.float32)
                for r in rights
            ],
            axis=1,
        )

    own_blocks = [me * blk_dev + b for b in range(blk_dev)]
    chip_blocks = [chip * blk_chip + b for b in range(blk_chip)]

    def hop(step, carry):
        greet(near.at[step])
        pl.semaphore_wait(near.at[step], known)
        return carry

    density = jnp.zeros((1, rows), jnp.float32)
    own = slab[core]
    for j in range(blk_chip):
        c, b = divmod(j, blk_dev)
        t = terms(slab[c, pl.ds(b * BLOCK, BLOCK), :], own)
        density = density + jnp.sum(t, axis=0, keepdims=True) * same(chip_blocks[j], own_blocks)

    lax.fori_loop(0, near.shape[0], hop, 0)

    def return_copy(d):
        return pltpu.make_async_remote_copy(
            src_ref=ret.at[d - 1],
            dst_ref=part.at[d - 1],
            send_sem=ret_send.at[d - 1],
            recv_sem=part_recv.at[d - 1],
            device_id=at(source(d), core),
            device_id_type=MESH,
        )

    def part_arrives(d):
        return pltpu.make_async_remote_copy(
            src_ref=ret.at[d - 1],
            dst_ref=part.at[d - 1],
            send_sem=ret_send.at[d - 1],
            recv_sem=part_recv.at[d - 1],
            device_id=at(target(d), core),
            device_id_type=MESH,
        )

    for b, d in steps:
        @pl.when(inside(source(d)) & needed(d, b))
        def _():
            row_copy(d, b).wait_recv()
            span = pl.ds(b * BLOCK, BLOCK)
            their = source(d) * blk_chip + core * blk_dev + b
            whole = slab[...].reshape(n_pair * rows, width)
            t = terms(normal(rx[d - 1, span, :]), whole) * same(their, chip_blocks)
            down = jnp.sum(t, axis=0, keepdims=True)
            for c in range(n_pair):
                acc[c] += down[:, c * rows:(c + 1) * rows]
            fold = sum(t[:, j * BLOCK:(j + 1) * BLOCK] for j in range(blk_chip))
            ret[d - 1, :, span] = jnp.sum(fold.T, axis=0, keepdims=True)

        if b == blk_dev - 1:
            @pl.when(inside(source(d)))
            def _():
                return_copy(d).start()

    mate_part = pltpu.make_async_remote_copy(
        src_ref=acc.at[mate],
        dst_ref=part.at[n_sub],
        send_sem=ret_send.at[n_sub],
        recv_sem=part_recv.at[n_sub],
        device_id=at(chip, mate),
        device_id_type=MESH,
    )
    mate_part.start()
    density = density + acc[core]
    mate_part.wait_recv()
    for d in range(1, n_sub + 1):
        @pl.when(inside(target(d)))
        def _():
            part_arrives(d).wait_recv()
    for d in range(n_sub + 1):
        density = density + part[d]
    dens_ref[...] = density

    weight = 1.0 / density
    lane = lax.broadcasted_iota(jnp.int32, (1, rows), 1)
    hi = weight.astype(jnp.bfloat16).astype(jnp.float32)
    mid = (weight - hi).astype(jnp.bfloat16).astype(jnp.float32)
    low = weight - hi - mid
    left = jnp.concatenate(
        [
            jnp.where(lane // BLOCK == b, piece, 0.0)
            for piece in (hi, mid, low)
            for b in range(blk_dev)
        ],
        axis=0,
    ).astype(jnp.bfloat16)
    sums = jnp.dot(left, own, preferred_element_type=jnp.float32)
    sums = (
        sums[0:blk_dev] + sums[blk_dev:2 * blk_dev] + sums[2 * blk_dev:3 * blk_dev]
    )
    totals = jnp.concatenate(
        [
            jnp.sum(weight[:, b * BLOCK:(b + 1) * BLOCK], axis=1, keepdims=True)
            for b in range(blk_dev)
        ],
        axis=0,
    )
    for s in range(n_sub):
        column = lax.broadcasted_iota(jnp.int32, (blk_dev, lanes), 1) + (lows[s] - s * feature_width)
        mine = (column >= 0) & (column < feature_width)
        msg[s] = jnp.where(mine, sums[:, lows[s]:lows[s] + lanes], totals)

    def spread(far, carry):
        to_run = lax.rem(run + far, n_runs)
        for x in range(n_sub):
            to_sub = lax.rem(sub + x, n_sub)
            for c in range(n_pair):
                if isinstance(far, int) and x + c == 0:
                    continue
                pltpu.make_async_remote_copy(
                    src_ref=msg.at[to_sub],
                    dst_ref=gathered.at[me],
                    send_sem=msg_send,
                    recv_sem=msg_recv,
                    device_id={"runs": to_run, "sub": to_sub, "pair": lax.rem(core + c, n_pair)},
                    device_id_type=MESH,
                ).start()
        return carry

    lax.fori_loop(1, n_runs, spread, 0, unroll=min(3, n_runs - 1))
    spread(0, 0)
    gathered[me] = msg[sub]

    mate_copy.wait_send()
    mate_part.wait_send()
    for b, d in steps:
        @pl.when(inside(target(d)) & needed(d, b))
        def _():
            row_copy(d, b).wait_send()
    for d in range(1, n_sub + 1):
        @pl.when(inside(source(d)))
        def _():
            return_copy(d).wait_send()

    most = gathered.at[pl.ds(0, count - 1)]
    pltpu.make_async_copy(most, most, msg_recv).wait()

    slot_row = lax.broadcasted_iota(jnp.int32, (8, 1), 0) + run * slots

    def place(q, total):
        got = gathered[q]
        for b in range(blk_dev):
            slot = owner_ref[ids_ref[q * blk_dev + b]]
            total = total + jnp.where(slot_row == slot, got[b:b + 1, :], 0.0)
        return total

    total = lax.fori_loop(
        0, count, place, jnp.zeros((8, lanes), jnp.float32), unroll=8
    )
    weights = jnp.where(sub == 0, total[:, feature_width:feature_width + 1], total[:, 0:1])
    proto_ref[...] = (total / weights)[0:slots]
    pltpu.make_async_copy(most, most, msg_send).wait()


def per_device(sizes, embeddings, block_cluster, owner):
    n_runs, n_sub, n_pair, blk_dev, lows, lanes, slots = sizes
    rows, width = embeddings.shape
    count = n_runs * n_sub * n_pair
    vmem = pl.BlockSpec(memory_space=pltpu.VMEM)
    hops = -(-(n_runs * n_sub - 1) // n_sub)
    density, wide = pl.pallas_call(
        functools.partial(kernel, sizes),
        out_shape=(
            jax.ShapeDtypeStruct((1, rows), jnp.float32),
            jax.ShapeDtypeStruct((slots, lanes), jnp.float32),
        ),
        in_specs=[pl.BlockSpec(memory_space=pl.ANY)] * 3,
        out_specs=(vmem, vmem),
        scratch_shapes=[
            pltpu.VMEM((rows, width), jnp.bfloat16),
            pltpu.SMEM(block_cluster.shape, jnp.int32),
            pltpu.SMEM(owner.shape, jnp.int32),
            pltpu.VMEM((n_pair, rows, width), jnp.bfloat16),
            pltpu.VMEM((n_sub, rows, width), jnp.bfloat16),
            pltpu.VMEM((n_pair, 1, rows), jnp.float32),
            pltpu.VMEM((n_sub, 1, rows), jnp.float32),
            pltpu.VMEM((n_sub + 1, 1, rows), jnp.float32),
            pltpu.VMEM((n_sub, blk_dev, lanes), jnp.float32),
            pltpu.VMEM((count, blk_dev, lanes), jnp.float32),
            pltpu.SemaphoreType.DMA((blk_dev + 2,)),
            pltpu.SemaphoreType.REGULAR((hops,)),
            pltpu.SemaphoreType.DMA,
            pltpu.SemaphoreType.DMA,
            pltpu.SemaphoreType.DMA((n_sub, blk_dev)),
            pltpu.SemaphoreType.DMA((n_sub, blk_dev)),
            pltpu.SemaphoreType.DMA((n_sub + 1,)),
            pltpu.SemaphoreType.DMA((n_sub + 1,)),
            pltpu.SemaphoreType.DMA,
            pltpu.SemaphoreType.DMA,
        ],
        compiler_params=pltpu.CompilerParams(
            collective_id=0, has_side_effects=True, vmem_limit_bytes=32 * 1024 * 1024
        ),
    )(embeddings, block_cluster, owner)
    sub = lax.axis_index("sub")
    feature_width = width // n_sub
    offset = sub * feature_width - jnp.asarray(lows, jnp.int32)[sub]
    return (density.reshape(rows), lax.dynamic_slice_in_dim(wide, offset, feature_width, 1))


def solution(mesh):
    placed = (P(("groups", "runs", "sub", "pair"), None), P("groups"), P("groups"))

    def whole(embeddings, block_cluster, owner):
        n_runs, n_sub, n_pair = (mesh.shape[a] for a in ("runs", "sub", "pair"))
        groups = mesh.shape["groups"]
        rows = embeddings.shape[0] // mesh.size
        width = embeddings.shape[1]
        feature_width = width // n_sub
        spans = [
            (s * feature_width // 128 * 128, -(-((s + 1) * feature_width) // 128) * 128)
            for s in range(n_sub)
        ]
        lanes = max(hi - lo for lo, hi in spans)
        assert lanes > feature_width, feature_width
        lows = tuple(min(lo, width - lanes) for lo, _ in spans)
        slots = owner.shape[0] // groups // n_runs
        sizes = (n_runs, n_sub, n_pair, rows // BLOCK, lows, lanes, slots)
        return jax.shard_map(
            functools.partial(per_device, sizes),
            mesh=mesh,
            in_specs=placed,
            out_specs=(P(("groups", "runs", "sub", "pair")), P(("groups", "runs"), "sub")),
            check_vma=False,
        )(embeddings, block_cluster, owner)

    return whole
```
